32 devices in a mesh: parts: 2 (over x), seq: 8 (over z, y), tp: 2 (over core).
Axes of the slice: x: 2, y: 2, z: 4, core: 2. Of those that a mesh axis runs over, the one named last changes fastest.
Arguments:
- video_q: bfloat16 [4096, 1024], P(('parts', 'seq', 'tp')), parts along dimension 0, may hold values from -6 to 6
- video_k: bfloat16 [4096, 1024], P(('parts', 'seq', 'tp')), parts along dimension 0, may hold values from -6 to 6
- video_v: bfloat16 [4096, 1024], P(('parts', 'seq', 'tp')), parts along dimension 0, may hold values from -6 to 6
- cross_q: bfloat16 [4096, 1024], P(('parts', 'seq', 'tp')), parts along dimension 0, may hold values from -6 to 6
- qk_gains: float32 [4, 1024], replicated, may hold values from 1 to 2
- captions: bfloat16 [4096, 4096], P(('parts', 'seq'), 'tp'), parts along dimension 0, may hold values from -16 to 16
- text_gain: float32 [4096], P('tp'), may hold values from 0.25 to 1.75
- cross_kv_weight: bfloat16 [4096, 2, 1024], P('tp', None, 'seq'), may hold values from -0.09375 to 0.09375
- lengths: int32 [8], P('parts'), parts along dimension 0, may hold values from 1 to 512, 1024 in all
- video_prompt: int32 [8], P('parts'), parts along dimension 0, may hold values from 0 to 3, each once
Outputs:
- self_out: bfloat16 [4096, 1024], P(('parts', 'seq', 'tp')), parts along dimension 0
- cross_out: bfloat16 [4096, 1024], P(('parts', 'seq', 'tp')), parts along dimension 0
The draws below stay inside these ranges and needn't reach their ends.
There are 2 independent parts, one for each index of `parts`. The reference program is written for one: setup_inputs(seed, part) draws one part's arguments, and reference() takes and returns one part's arrays. A program takes and returns all parts, laid end to end along the dimension named above; an argument that names none is the same for every part. Nothing has to cross between parts.
Inputs may be any that keep to these rules, and one draw needn't show every extreme that they name: The lengths of a group's captions add up to 1024, and one caption has exactly 512. `video_prompt`: every caption belongs to exactly one video.
All inputs are finite; a program needn't handle non-finite values.
Results may differ from the reference program's by a relative error of at most 0.011.
Values may be sent and summed in bfloat16 or wider, within the bound.
A program may use at most 128 MiB of HBM per device.

```python
import math
import jax
import jax.numpy as jnp
import numpy as np
from jax import lax

DT = 4096
HD = 128
HEADS = 8
DM = 1024
VIDEOS = 4
PROMPTS = 4
CAP = 512
CAP_VALID = 1024
TOKENS = 2048


def draw_captions(key, part):
    noise_key = jax.random.fold_in(key, 0)
    values = jax.random.normal(noise_key, (PROMPTS * CAP, DT), jnp.float32)
    return jnp.clip(values, -16.0, 16.0).astype(jnp.bfloat16)


def shard_levels(key, extent, shards, low, top_value):
    level, own = 1.0, jax.random.fold_in(key, 6)
    for position, shards_of in shards:
        draws = jnp.exp(jax.random.uniform(jax.random.fold_in(own, position), (shards_of,), jnp.float32, low / len(shards), top_value / len(shards)))
        level = level * jnp.repeat(draws, extent[position] // shards_of).reshape([-1 if axis == position else 1 for axis in range(len(extent))])
    return level


def profile(count, total, most, lean):
    loads = [(1 << 20) // math.isqrt(rank ** lean) + 1 for rank in range(2, count + 1)]
    spare, holding = total - most - (count - 1), [1] * (count - 1)
    while spare > 0:
        candidates = [i for i in range(count - 1) if holding[i] < most]
        mass, left = sum([loads[i] for i in candidates]), spare
        for i in candidates:
            extra = min(most - holding[i], max(1, left * loads[i] // mass), spare)
            holding[i] = holding[i] + extra
            spare = spare - extra
    return np.array([most] + holding)


def ragged(own_key, number_of, total, most, lean):
    if number_of == 2:
        one = jax.random.randint(own_key, (), max(1, total - most), min(most, total - 1) + 1)
        return jnp.stack([one, total - one])
    tallies = jnp.asarray(profile(number_of, total, most, lean), jnp.int32)
    pairs = (number_of - 1) // 2
    giver, receiver = tallies[1:1 + 2 * pairs:2], tallies[2:2 + 2 * pairs:2]
    margin = jnp.minimum(giver - 1, most - receiver)
    shifted = jax.random.randint(jax.random.fold_in(own_key, 1), (pairs,), 0, 1 << 20) % (margin + 1)
    tallies = tallies.at[1:1 + 2 * pairs:2].set(giver - shifted).at[2:2 + 2 * pairs:2].set(receiver + shifted)
    return tallies[jax.random.permutation(jax.random.fold_in(own_key, 2), number_of)]


def bell_draw(own_key, dims, scale, bound, cuts=(), kind=jnp.bfloat16):
    result = scale * jax.random.normal(own_key, dims, jnp.float32)
    if cuts:
        result = result * shard_levels(own_key, dims, cuts, -0.22, 0.18)
    return jnp.clip(result, -bound, bound).astype(kind)


def setup_inputs(seed: int = 0, part: int = 0) -> dict:
    seeds = jax.random.split(jax.random.key(seed), 11)
    own_keys = jax.random.split(jax.random.fold_in(seeds[10], part), 11)
    video_q = bell_draw(own_keys[0], (TOKENS, DM), 1.0, 6.0, ((0, 16),))
    video_k = bell_draw(own_keys[1], (TOKENS, DM), 1.0, 6.0, ((0, 16),))
    video_v = bell_draw(own_keys[2], (TOKENS, DM), 1.0, 6.0, ((0, 16),))
    cross_q = bell_draw(own_keys[3], (TOKENS, DM), 1.0, 6.0, ((0, 16),))
    qk_gains = jnp.clip(jnp.exp(jax.random.uniform(seeds[4], (4, DM), jnp.float32, math.log(1.0), math.log(2.0))), 1.0, 2.0)
    captions = draw_captions(jax.random.fold_in(jax.random.fold_in(seeds[10], part), 71), part)
    text_gain = jnp.clip(1.0 + 0.15 * jax.random.normal(seeds[6], (DT,), jnp.float32), 0.25, 1.75)
    cross_kv_weight = bell_draw(seeds[7], (DT, 2, DM), DT ** -0.5, 0.09375, ((0, 2), (2, 8)))
    lengths = ragged(own_keys[8], PROMPTS, CAP_VALID, CAP, 2).astype(jnp.int32)
    video_prompt = jax.random.permutation(own_keys[9], PROMPTS).astype(jnp.int32)
    return {"video_q": video_q, "video_k": video_k, "video_v": video_v, "cross_q": cross_q, "qk_gains": qk_gains, "captions": captions, "text_gain": text_gain, "cross_kv_weight": cross_kv_weight, "lengths": lengths, "video_prompt": video_prompt}


EPS = 1e-06

def head_norm(values, gain):
    inverse = lax.rsqrt(lax.optimization_barrier(jnp.mean(values * values, axis=-1, keepdims=True)) + EPS)
    return values * inverse * gain

def reference(video_q, video_k, video_v, cross_q, qk_gains, captions, text_gain, cross_kv_weight, lengths, video_prompt):
    text_rows = captions.astype(jnp.float32)
    inverse = lax.rsqrt(lax.optimization_barrier(jnp.mean(text_rows * text_rows, axis=1, keepdims=True)) + EPS)
    text_normed = (text_rows * inverse * text_gain[None, :]).astype(jnp.bfloat16)
    weight = cross_kv_weight.reshape(DT, 2 * HEADS * HD)
    key_value = jnp.dot(text_normed, weight, preferred_element_type=jnp.float32).reshape(PROMPTS, CAP, 2, HEADS, HD)
    head_gains = qk_gains.astype(jnp.float32).reshape(4, HEADS, HD)
    cross_keys = head_norm(key_value[:, :, 0], head_gains[3]).astype(jnp.bfloat16)
    cross_values = key_value[:, :, 1].astype(jnp.bfloat16)
    chosen_keys = jnp.transpose(cross_keys[video_prompt], (2, 0, 1, 3))
    chosen_values = jnp.transpose(cross_values[video_prompt], (2, 0, 1, 3))
    visible = jnp.arange(CAP, dtype=jnp.int32)[None, :] < lengths[video_prompt][:, None]

    def prepare(rows, gain):
        shaped = rows.astype(jnp.float32).reshape(TOKENS, HEADS, HD)
        return jnp.transpose(head_norm(shaped, gain).astype(jnp.bfloat16), (1, 0, 2))
    self_queries = prepare(video_q, head_gains[0])
    self_keys = prepare(video_k, head_gains[1])
    cross_queries = prepare(cross_q, head_gains[2])
    head_values = jnp.transpose(video_v.reshape(TOKENS, HEADS, HD), (1, 0, 2))
    score_scale = 1.0 / math.sqrt(HD)
    video_len = TOKENS // VIDEOS

    def one_head(operands):
        queries, key_rows, value_rows, cross_rows, cap_keys, cap_values = operands
        queries = queries.reshape(VIDEOS, video_len, HD).astype(jnp.float32)
        key_rows = key_rows.reshape(VIDEOS, video_len, HD).astype(jnp.float32)
        value_rows = value_rows.reshape(VIDEOS, video_len, HD).astype(jnp.float32)
        cross_rows = cross_rows.reshape(VIDEOS, video_len, HD).astype(jnp.float32)
        scores = jnp.einsum('vqd,vkd->vqk', queries, key_rows) * score_scale
        exp_scores = jnp.exp(scores)
        weights = (exp_scores / lax.optimization_barrier(jnp.sum(exp_scores, axis=2, keepdims=True))).astype(jnp.bfloat16)
        self_part = jnp.einsum('vqk,vkd->vqd', weights.astype(jnp.float32), value_rows).astype(jnp.bfloat16)
        cross_scores = jnp.einsum('vqd,vkd->vqk', cross_rows, cap_keys.astype(jnp.float32)) * score_scale
        cross_exp = jnp.where(visible[:, None, :], jnp.exp(cross_scores), 0.0)
        cross_weights = (cross_exp / lax.optimization_barrier(jnp.sum(cross_exp, axis=2, keepdims=True))).astype(jnp.bfloat16)
        cross_part = jnp.einsum('vqk,vkd->vqd', cross_weights.astype(jnp.float32), cap_values.astype(jnp.float32)).astype(jnp.bfloat16)
        return (self_part.reshape(TOKENS, HD), cross_part.reshape(TOKENS, HD))
    self_heads, cross_heads = lax.map(one_head, (self_queries, self_keys, head_values, cross_queries, chosen_keys, chosen_values))
    self_out = jnp.transpose(self_heads, (1, 0, 2)).reshape(TOKENS, HEADS * HD)
    cross_out = jnp.transpose(cross_heads, (1, 0, 2)).reshape(TOKENS, HEADS * HD)
    return (self_out, cross_out)
```

```python
import functools
import math

import jax
import jax.numpy as jnp
from jax import lax
from jax.experimental import pallas as pl
from jax.experimental.pallas import tpu as pltpu
from jax.sharding import PartitionSpec as P

EPS = 1e-06
MESH = pl.DeviceIdType.MESH
F32, BF16 = jnp.float32, jnp.bfloat16


def head_norm(rows, gain):
    values = rows.astype(F32)
    inverse = lax.rsqrt(jnp.mean(values * values, axis=-1, keepdims=True) + EPS)
    return (values * inverse * gain).astype(BF16)


def kernel(
    dims, q_ref, k_ref, v_ref, cq_ref, gains_ref, cap_ref, tg_ref, w_ref, len_ref, vp_ref,
    self_ref, cross_ref,
    wbuf, capbuf, ssbuf, tn, pb, prb, kvs, kvbuf, sbuf, kn, sost, sob, cqbuf, qn, cost, cob,
    w_send, w_recv, f_send, cap_send, cap_recv, ss_send, ss_recv, p_send, p_recv,
    kv_send, kv_recv, kf_send, self_send, self_recv, cq_send, cq_recv,
    so_send, so_recv, co_send, co_recv, loc_sem,
):
    parts, n, T, V = dims
    gr = n // V
    G = gr * T
    p, s, c = lax.axis_index("parts"), lax.axis_index("seq"), lax.axis_index("tp")
    v, r = lax.div(s, gr), lax.rem(s, gr)
    g = r * T + c
    R, DM = q_ref.shape
    CR, FH = cap_ref.shape
    HD = DM // n
    HC = DM // G
    HL = HC // HD
    PR = FH // parts
    ROWS = gr * CR
    HR = ROWS // T
    scale = 1.0 / math.sqrt(HD)

    def mod(a, m):
        return lax.rem(a, m)

    def rc(src, dst, ss, rs, dev):
        return pltpu.make_async_remote_copy(
            src_ref=src, dst_ref=dst, send_sem=ss, recv_sem=rs, device_id=dev, device_id_type=MESH
        )

    def cols(i, width):
        return pl.ds(pl.multiple_of(i * width, width), width)

    def prow(i):
        return pl.ds(pl.multiple_of(i * PR, PR), PR)

    barrier = pltpu.get_barrier_semaphore()
    greeted = [(p, mod(s + d, n), c) for d in range(1, n)]
    greeted += [(p, v * gr + x, mod(c + d, T)) for x in range(gr) for d in range(1, T)]
    greeted += [(mod(p + d, parts), s, c) for d in range(1, parts)]
    for dev in greeted:
        pl.semaphore_signal(barrier, inc=1, device_id=dev, device_id_type=MESH)
    pl.semaphore_wait(barrier, len(greeted))

    pending = []

    def go(copy):
        copy.start()
        pending.append(copy)

    for d in range(1, V):
        go(rc(w_ref.at[prow(p)], wbuf.at[v, prow(p)], w_send.at[d], w_recv.at[v, p],
              (p, mod(v + d, V) * gr + r, c)))
    for d in range(1, gr):
        go(rc(cap_ref, capbuf.at[r], cap_send.at[d], cap_recv.at[r],
              (p, v * gr + mod(r + d, gr), c)))
    own = []
    for a, ref in enumerate((q_ref, k_ref, v_ref)):
        for d in range(1, G):
            gg = mod(g + d, G)
            go(rc(ref.at[:, cols(gg, HC)], sbuf.at[a, g], self_send.at[a, d], self_recv.at[a, g],
                  (p, v * gr + lax.div(gg, T), mod(gg, T))))
        own.append(pltpu.make_async_copy(ref.at[:, cols(g, HC)], sbuf.at[a, g], loc_sem.at[a]))
    own.append(pltpu.make_async_copy(cq_ref.at[:, cols(s, HD)], cqbuf.at[s], loc_sem.at[3]))
    for copy in own:
        copy.start()
    for d in range(1, n):
        t = mod(s + d, n)
        go(rc(cq_ref.at[:, cols(t, HD)], cqbuf.at[s], cq_send.at[d], cq_recv.at[s], (p, t, c)))

    def wait_in(dst, sem):
        rc(dst, dst, loc_sem.at[4], sem, (p, mod(s + 1, n), c)).wait_recv()

    CH = 16

    def squares(src, row0):
        def step(i, carry):
            x = src[pl.ds(pl.multiple_of(i * CH, CH), CH), :].astype(F32)
            total = jnp.sum(x * x, axis=1, keepdims=True)
            ssbuf[c, pl.ds(pl.multiple_of(row0 + i * CH, CH), CH), :] = jnp.broadcast_to(total, (CH, 128))
            return carry
        lax.fori_loop(0, CR // CH, step, 0)

    def normalize(src, row0):
        def step(i, carry):
            x = src[pl.ds(pl.multiple_of(i * CH, CH), CH), :].astype(F32)
            rows = pl.ds(pl.multiple_of(row0 + i * CH, CH), CH)
            total = ssbuf[0, rows, :]
            for t in range(1, T):
                total = total + ssbuf[t, rows, :]
            inverse = lax.rsqrt(total[:, :1] / (FH * T) + EPS)
            tn[rows, :] = (x * inverse * tg_ref[...]).astype(BF16)
            return carry
        lax.fori_loop(0, CR // CH, step, 0)

    squares(cap_ref, r * CR)
    for d in range(1, gr):
        rr = mod(r + d, gr)
        wait_in(capbuf.at[rr], cap_recv.at[rr])
        squares(capbuf.at[rr], rr * CR)
    for d in range(1, T):
        go(rc(ssbuf.at[c], ssbuf.at[c], ss_send.at[d], ss_recv.at[c], (p, s, mod(c + d, T))))

    for copy in own:
        copy.wait()
    for a in (1, 0, 2):
        for d in range(1, G):
            gg = mod(g + d, G)
            wait_in(sbuf.at[a, gg], self_recv.at[a, gg])
    for j in range(HL):
        js = slice(j * HD, (j + 1) * HD)
        gain = gains_ref[1:2, cols(g * HL + j, HD)]

        def knorm(i, carry):
            kn[i, :, js] = head_norm(sbuf[1, i, :, js], gain)
            return carry
        lax.fori_loop(0, G, knorm, 0)

    def attend_self(gg):
        for j in range(HL):
            js = slice(j * HD, (j + 1) * HD)
            gain = gains_ref[0:1, cols(g * HL + j, HD)]
            queries = head_norm(sbuf[0, gg, :, js], gain)
            keys = kn[:, :, js].reshape(G * R, HD)
            scores = lax.dot_general(queries, keys, (((1,), (1,)), ((), ())),
                                     preferred_element_type=F32)
            e = jnp.exp(scores * scale)
            total = jnp.sum(e, axis=1, keepdims=True)
            values = sbuf[2, :, :, js].reshape(G * R, HD)
            o = jnp.dot(e.astype(BF16), values, preferred_element_type=F32) / total
            sost[gg, :, js] = o.astype(BF16)

    def self_step(i, carry):
        gg = mod(g + 1 + i, G)
        attend_self(gg)
        rc(sost.at[gg], sob.at[:, cols(g, HC)], so_send.at[gg], so_recv.at[g],
           (p, v * gr + lax.div(gg, T), mod(gg, T))).start()
        return carry
    lax.fori_loop(0, G - 1, self_step, 0)
    attend_self(g)
    sob[:, cols(g, HC)] = sost[g]

    for d in range(1, V):
        vv = mod(v + d, V)
        wait_in(wbuf.at[vv, prow(p)], w_recv.at[vv, p])
        for e in range(1, parts):
            go(rc(wbuf.at[vv, prow(p)], wbuf.at[vv, prow(p)], f_send.at[d, e], w_recv.at[vv, p],
                  (mod(p + e, parts), s, c)))

    for d in range(1, T):
        cc = mod(c + d, T)
        wait_in(ssbuf.at[cc], ss_recv.at[cc])
    normalize(cap_ref, r * CR)
    for d in range(1, gr):
        rr = mod(r + d, gr)
        normalize(capbuf.at[rr], rr * CR)

    for d in range(1, n):
        t = mod(s + d, n)
        wait_in(cqbuf.at[t], cq_recv.at[t])
    cross_gain = gains_ref[2:3, cols(s, HD)]

    def qnorm(i, carry):
        qn[i] = head_norm(cqbuf[i], cross_gain)
        return carry
    lax.fori_loop(0, n, qnorm, 0)

    for d in range(V):
        vv = mod(v + d, V)
        if d == 0:
            weight = w_ref[...]
        else:
            for e in range(1, parts):
                pp = mod(p + e, parts)
                wait_in(wbuf.at[vv, prow(pp)], w_recv.at[vv, pp])
            weight = wbuf[vv]
        for e in range(1, T + 1):
            cc = mod(c + e, T)
            rows = pl.ds(pl.multiple_of(cc * HR, HR), HR)
            pb[d, cc] = jnp.dot(tn[rows, :], weight, preferred_element_type=F32)
            if e < T:
                go(rc(pb.at[d, cc], prb.at[d, c], p_send.at[d, e], p_recv.at[d, c], (p, s, cc)))
        total = pb[d, c]
        for e in range(1, T):
            cc = mod(c + e, T)
            wait_in(prb.at[d, cc], p_recv.at[d, cc])
            total = total + prb[d, cc]
        gain = gains_ref[3:4, cols(vv * gr + r, HD)]
        keys = head_norm(total[:, :HD], gain)
        values = total[:, HD:].astype(BF16)
        if d == 0:
            kvbuf[v, c, :, :HD] = keys
            kvbuf[v, c, :, HD:] = values
            for e in range(1, T):
                go(rc(kvbuf.at[v, c], kvbuf.at[v, c], kf_send.at[d, e], kv_recv.at[v, c],
                      (p, s, mod(c + e, T))))
        else:
            kvs[d, :, :HD] = keys
            kvs[d, :, HD:] = values
            go(rc(kvs.at[d], kvbuf.at[v, c], kv_send.at[d], kv_recv.at[v, c],
                  (p, vv * gr + r, c)))
    for d in range(1, V):
        vv = mod(v + V - d, V)
        wait_in(kvbuf.at[vv, c], kv_recv.at[vv, c])
        for e in range(1, T):
            go(rc(kvbuf.at[vv, c], kvbuf.at[vv, c], kf_send.at[d, e], kv_recv.at[vv, c],
                  (p, s, mod(c + e, T))))
    for d in range(V):
        vv = mod(v + V - d, V)
        for e in range(1, T):
            cc = mod(c + e, T)
            wait_in(kvbuf.at[vv, cc], kv_recv.at[vv, cc])

    def attend_cross(vv):
        prompt = vp_ref[vv]
        length = len_ref[prompt]
        kv = kvbuf[prompt].reshape(ROWS, 2 * HD)
        queries = qn[pl.ds(vv * gr, gr)].reshape(gr * R, HD)
        scores = lax.dot_general(queries, kv[:, :HD], (((1,), (1,)), ((), ())),
                                 preferred_element_type=F32)
        visible = lax.broadcasted_iota(jnp.int32, (1, ROWS), 1) < length
        e = jnp.where(visible, jnp.exp(scores * scale), 0.0)
        total = jnp.sum(e, axis=1, keepdims=True)
        o = jnp.dot(e.astype(BF16), kv[:, HD:], preferred_element_type=F32) / total
        cost[pl.ds(vv * gr, gr)] = o.astype(BF16).reshape(gr, R, HD)

    def co_copy(t):
        return rc(cost.at[t], cob.at[:, cols(s, HD)], co_send.at[t], co_recv.at[s], (p, t, c))

    def cross_step(i, carry):
        vv = mod(v + 1 + i, V)
        attend_cross(vv)
        for x in range(gr):
            co_copy(vv * gr + x).start()
        return carry
    lax.fori_loop(0, V - 1, cross_step, 0)
    attend_cross(v)
    for d in range(1, gr):
        co_copy(v * gr + mod(r + d, gr)).start()
    cob[:, cols(s, HD)] = cost[s]

    for d in range(1, G):
        gg = mod(g + d, G)
        wait_in(sob.at[:, cols(gg, HC)], so_recv.at[gg])
    self_ref[...] = sob[...]
    for d in range(1, n):
        t = mod(s + d, n)
        wait_in(cob.at[:, cols(t, HD)], co_recv.at[t])
    cross_ref[...] = cob[...]

    for copy in pending:
        copy.wait_send()
    for d in range(1, G):
        gg = mod(g + d, G)
        rc(sost.at[gg], sob.at[:, cols(g, HC)], so_send.at[gg], so_recv.at[g],
           (p, v * gr + lax.div(gg, T), mod(gg, T))).wait_send()
    for d in range(1, n):
        co_copy(mod(s + d, n)).wait_send()


def per_device(
    video_q, video_k, video_v, cross_q, qk_gains, captions, text_gain, cross_kv_weight,
    lengths, video_prompt,
):
    parts, n, T = (lax.axis_size(a) for a in ("parts", "seq", "tp"))
    V = lengths.shape[0]
    gr = n // V
    G = gr * T
    R, DM = video_q.shape
    CR, FH = captions.shape
    HD = DM // n
    HC = DM // G
    ROWS = gr * CR
    HR = ROWS // T
    weight = cross_kv_weight.reshape(FH, 2 * HD)
    vm = pl.BlockSpec(memory_space=pltpu.VMEM)
    sm = pl.BlockSpec(memory_space=pltpu.SMEM)
    sem = pltpu.SemaphoreType.DMA
    VM = pltpu.VMEM
    return pl.pallas_call(
        functools.partial(kernel, (parts, n, T, V)),
        out_shape=(
            jax.ShapeDtypeStruct((R, DM), BF16),
            jax.ShapeDtypeStruct((R, DM), BF16),
        ),
        in_specs=[vm] * 8 + [sm] * 2,
        out_specs=(vm, vm),
        scratch_shapes=[
            VM((V, FH, 2 * HD), BF16),
            VM((gr, CR, FH), BF16),
            VM((T, ROWS, 128), F32),
            VM((ROWS, FH), BF16),
            VM((V, T, HR, 2 * HD), F32),
            VM((V, T, HR, 2 * HD), F32),
            VM((V, HR, 2 * HD), BF16),
            VM((V, T, HR, 2 * HD), BF16),
            VM((3, G, R, HC), BF16),
            VM((G, R, HC), BF16),
            VM((G, R, HC), BF16),
            VM((R, DM), BF16),
            VM((n, R, HD), BF16),
            VM((n, R, HD), BF16),
            VM((n, R, HD), BF16),
            VM((R, DM), BF16),
            sem((V,)), sem((V, parts)), sem((V, parts)),
            sem((gr,)), sem((gr,)),
            sem((T,)), sem((T,)),
            sem((V, T)), sem((V, T)),
            sem((V,)), sem((V, T)), sem((V, T)),
            sem((3, G)), sem((3, G)),
            sem((n,)), sem((n,)),
            sem((G,)), sem((G,)),
            sem((n,)), sem((n,)),
            sem((5,)),
        ],
        compiler_params=pltpu.CompilerParams(
            collective_id=0, has_side_effects=True, vmem_limit_bytes=56 * 1024 * 1024
        ),
    )(
        video_q, video_k, video_v, cross_q, qk_gains, captions, text_gain.reshape(1, FH), weight,
        lengths, video_prompt,
    )


def solution(mesh):
    rows = P(("parts", "seq", "tp"), None)
    return jax.shard_map(
        per_device,
        mesh=mesh,
        in_specs=(
            rows, rows, rows, rows, P(), P(("parts", "seq"), "tp"), P("tp"),
            P("tp", None, "seq"), P("parts"), P("parts"),
        ),
        out_specs=(rows, rows),
        check_vma=False,
    )
```

```python
import functools
import math

import jax
import jax.numpy as jnp
from jax import lax
from jax.experimental import pallas as pl
from jax.experimental.pallas import tpu as pltpu
from jax.sharding import PartitionSpec as P

EPS = 1e-06
MESH = pl.DeviceIdType.MESH
F32, BF16 = jnp.float32, jnp.bfloat16
Q = 2


def head_norm(rows, gain):
    values = rows.astype(F32)
    inverse = lax.rsqrt(jnp.mean(values * values, axis=-1, keepdims=True) + EPS)
    return (values * inverse * gain).astype(BF16)


def kernel(
    dims, q_ref, k_ref, v_ref, cq_ref, gains_ref, cap_ref, tg_ref, w_ref, len_ref, vp_ref,
    self_ref, cross_ref,
    wbuf, capbuf, ssbuf, tn, pb, prb, kvs, kvbuf, sbuf, kn, sost, sob, cqbuf, qn, cost, cob,
    wr_send, wl_send, w_recv, f_send, cap_send, cap_recv, ss_send, ss_recv, p_send, p_recv,
    kv_send, kv_recv, kf_send, self_send, self_recv, cq_send, cq_recv,
    so_send, so_recv, co_send, co_recv, loc_sem,
):
    parts, n, T, V = dims
    gr = n // V
    G = gr * T
    p, s, c = lax.axis_index("parts"), lax.axis_index("seq"), lax.axis_index("tp")
    v, r = lax.div(s, gr), lax.rem(s, gr)
    g = r * T + c
    R, DM = q_ref.shape
    CR, FH = cap_ref.shape
    HD = DM // n
    HC = DM // G
    HL = HC // HD
    PR = FH // (parts * Q)
    ROWS = gr * CR
    HR = ROWS // T
    scale = 1.0 / math.sqrt(HD)

    def mod(a, m):
        return lax.rem(a, m)

    def rc(src, dst, ss, rs, dev):
        return pltpu.make_async_remote_copy(
            src_ref=src, dst_ref=dst, send_sem=ss, recv_sem=rs, device_id=dev, device_id_type=MESH
        )

    def cols(i, width):
        return pl.ds(pl.multiple_of(i * width, width), width)

    def prow(i, q):
        return pl.ds(pl.multiple_of((i * Q + q) * PR, PR), PR)

    left_of, right_of = v, V - 1 - v
    both = jnp.minimum(left_of, right_of)

    def nearest(k):
        near = k // 2 + 1
        far = k - both + 1
        return jnp.where(
            k < 2 * both,
            v - near if k % 2 == 0 else v + near,
            jnp.where(left_of > right_of, v - far, v + far),
        )

    barrier = pltpu.get_barrier_semaphore()
    greeted = [(p, mod(s + d, n), c) for d in range(1, n)]
    greeted += [(p, v * gr + x, mod(c + d, T)) for x in range(gr) for d in range(1, T)]
    greeted += [(mod(p + d, parts), s, c) for d in range(1, parts)]
    for dev in greeted:
        pl.semaphore_signal(barrier, inc=1, device_id=dev, device_id_type=MESH)
    pl.semaphore_wait(barrier, len(greeted))

    pending = []

    def go(copy, when=None):
        pending.append((copy, when))
        if when is None:
            copy.start()
        else:
            pl.when(when)(copy.start)

    def wait_in(dst, sem):
        rc(dst, dst, loc_sem.at[4], sem, (p, mod(s + 1, n), c)).wait_recv()

    def pass_on(src, u, q, step, when):
        row = prow(p, q)
        target = jnp.clip(v + step, 0, V - 1) * gr + r
        sems = wr_send if step > 0 else wl_send
        go(rc(src, wbuf.at[u, row], sems.at[u, q], w_recv.at[u, p, q], (p, target, c)), when)

    for q in range(Q):
        pass_on(w_ref.at[prow(p, q)], v, q, 1, v + 1 < V)
        pass_on(w_ref.at[prow(p, q)], v, q, -1, v > 0)

    def weight_step(d):
        for q in range(Q):
            row = prow(p, q)
            for step in (1, -1):
                there = v - step * d
                here = (there >= 0) & (there < V)
                u = jnp.clip(there, 0, V - 1)

                @pl.when(here)
                def _():
                    wait_in(wbuf.at[u, row], w_recv.at[u, p, q])
                onward = here & ((v + step >= 0) & (v + step < V))
                pass_on(wbuf.at[u, row], u, q, step, onward)
                for e in range(1, parts):
                    go(rc(wbuf.at[u, row], wbuf.at[u, row], f_send.at[u, e, q],
                          w_recv.at[u, p, q], (mod(p + e, parts), s, c)), here)

    for d in range(1, gr):
        go(rc(cap_ref, capbuf.at[r], cap_send.at[d], cap_recv.at[r],
              (p, v * gr + mod(r + d, gr), c)))
    CH = 16

    def squares(src, row0):
        def step(i, carry):
            x = src[pl.ds(pl.multiple_of(i * CH, CH), CH), :].astype(F32)
            total = jnp.sum(x * x, axis=1, keepdims=True)
            ssbuf[c, pl.ds(pl.multiple_of(row0 + i * CH, CH), CH), :] = jnp.broadcast_to(total, (CH, 128))
            return carry
        lax.fori_loop(0, CR // CH, step, 0)

    def normalize(src, row0):
        def step(i, carry):
            x = src[pl.ds(pl.multiple_of(i * CH, CH), CH), :].astype(F32)
            rows = pl.ds(pl.multiple_of(row0 + i * CH, CH), CH)
            total = ssbuf[0, rows, :]
            for t in range(1, T):
                total = total + ssbuf[t, rows, :]
            inverse = lax.rsqrt(total[:, :1] / (FH * T) + EPS)
            tn[rows, :] = (x * inverse * tg_ref[...]).astype(BF16)
            return carry
        lax.fori_loop(0, CR // CH, step, 0)

    squares(cap_ref, r * CR)
    weight_step(1)
    for d in range(1, n):
        t = mod(s + d, n)
        go(rc(cq_ref.at[:, cols(t, HD)], cqbuf.at[s], cq_send.at[d], cq_recv.at[s], (p, t, c)))
    for d in range(2, V - 1):
        weight_step(d)
    for d in range(1, gr):
        rr = mod(r + d, gr)
        wait_in(capbuf.at[rr], cap_recv.at[rr])
        squares(capbuf.at[rr], rr * CR)
    for d in range(1, T):
        go(rc(ssbuf.at[c], ssbuf.at[c], ss_send.at[d], ss_recv.at[c], (p, s, mod(c + d, T))))
    own = []
    for a, ref in enumerate((q_ref, k_ref, v_ref)):
        for d in range(1, G):
            gg = mod(g + d, G)
            go(rc(ref.at[:, cols(gg, HC)], sbuf.at[a, g], self_send.at[a, d], self_recv.at[a, g],
                  (p, v * gr + lax.div(gg, T), mod(gg, T))))
        own.append(pltpu.make_async_copy(ref.at[:, cols(g, HC)], sbuf.at[a, g], loc_sem.at[a]))
    own.append(pltpu.make_async_copy(cq_ref.at[:, cols(s, HD)], cqbuf.at[s], loc_sem.at[3]))
    for copy in own:
        copy.start()
    for d in range(1, T):
        cc = mod(c + d, T)
        wait_in(ssbuf.at[cc], ss_recv.at[cc])
    normalize(cap_ref, r * CR)
    for d in range(1, gr):
        rr = mod(r + d, gr)
        normalize(capbuf.at[rr], rr * CR)

    def key_value_block(d):
        vv = v if d == 0 else nearest(d - 1)
        if d == 0:
            weight = w_ref[...]
        else:
            for e in range(1, parts):
                pp = mod(p + e, parts)
                for q in range(Q):
                    wait_in(wbuf.at[vv, prow(pp, q)], w_recv.at[vv, pp, q])
            weight = wbuf[vv]
        for e in range(1, T + 1):
            cc = mod(c + e, T)
            rows = pl.ds(pl.multiple_of(cc * HR, HR), HR)
            pb[d, cc] = jnp.dot(tn[rows, :], weight, preferred_element_type=F32)
            if e < T:
                go(rc(pb.at[d, cc], prb.at[d, c], p_send.at[d, e], p_recv.at[d, c], (p, s, cc)))
        total = pb[d, c]
        for e in range(1, T):
            cc = mod(c + e, T)
            wait_in(prb.at[d, cc], p_recv.at[d, cc])
            total = total + prb[d, cc]
        gain = gains_ref[3:4, cols(vv * gr + r, HD)]
        keys = head_norm(total[:, :HD], gain)
        values = total[:, HD:].astype(BF16)
        if d == 0:
            kvbuf[v, c, :, :HD] = keys
            kvbuf[v, c, :, HD:] = values
            for e in range(1, T):
                go(rc(kvbuf.at[v, c], kvbuf.at[v, c], kf_send.at[d, e], kv_recv.at[v, c],
                      (p, s, mod(c + e, T))))
        else:
            kvs[d, :, :HD] = keys
            kvs[d, :, HD:] = values
            go(rc(kvs.at[d], kvbuf.at[v, c], kv_send.at[d], kv_recv.at[v, c],
                  (p, vv * gr + r, c)))
    weight_step(V - 1)
    key_value_block(0)

    for copy in own:
        copy.wait()
    for a in (1, 0, 2):
        for d in range(1, G):
            gg = mod(g + d, G)
            wait_in(sbuf.at[a, gg], self_recv.at[a, gg])
    for j in range(HL):
        js = slice(j * HD, (j + 1) * HD)
        gain = gains_ref[1:2, cols(g * HL + j, HD)]

        def knorm(i, carry):
            kn[i, :, js] = head_norm(sbuf[1, i, :, js], gain)
            return carry
        lax.fori_loop(0, G, knorm, 0)

    def attend_self(gg):
        for j in range(HL):
            js = slice(j * HD, (j + 1) * HD)
            gain = gains_ref[0:1, cols(g * HL + j, HD)]
            queries = head_norm(sbuf[0, gg, :, js], gain)
            keys = kn[:, :, js].reshape(G * R, HD)
            scores = lax.dot_general(queries, keys, (((1,), (1,)), ((), ())),
                                     preferred_element_type=F32)
            e = jnp.exp(scores * scale)
            total = jnp.sum(e, axis=1, keepdims=True)
            values = sbuf[2, :, :, js].reshape(G * R, HD)
            o = jnp.dot(e.astype(BF16), values, preferred_element_type=F32) / total
            sost[gg, :, js] = o.astype(BF16)

    def self_step(i, carry):
        gg = mod(g + 1 + i, G)
        attend_self(gg)
        rc(sost.at[gg], sob.at[:, cols(g, HC)], so_send.at[gg], so_recv.at[g],
           (p, v * gr + lax.div(gg, T), mod(gg, T))).start()
        return carry
    lax.fori_loop(0, G - 1, self_step, 0)
    attend_self(g)
    sob[:, cols(g, HC)] = sost[g]

    for d in range(1, n):
        t = mod(s + d, n)
        wait_in(cqbuf.at[t], cq_recv.at[t])
    cross_gain = gains_ref[2:3, cols(s, HD)]

    def qnorm(i, carry):
        qn[i] = head_norm(cqbuf[i], cross_gain)
        return carry
    lax.fori_loop(0, n, qnorm, 0)

    for d in range(1, V):
        key_value_block(d)
    for d in range(1, V):
        vv = nearest(d - 1)
        wait_in(kvbuf.at[vv, c], kv_recv.at[vv, c])
        for e in range(1, T):
            go(rc(kvbuf.at[vv, c], kvbuf.at[vv, c], kf_send.at[d, e], kv_recv.at[vv, c],
                  (p, s, mod(c + e, T))))
    for d in range(V):
        vv = mod(v + V - d, V)
        for e in range(1, T):
            cc = mod(c + e, T)
            wait_in(kvbuf.at[vv, cc], kv_recv.at[vv, cc])

    def attend_cross(vv):
        prompt = vp_ref[vv]
        length = len_ref[prompt]
        kv = kvbuf[prompt].reshape(ROWS, 2 * HD)
        queries = qn[pl.ds(vv * gr, gr)].reshape(gr * R, HD)
        scores = lax.dot_general(queries, kv[:, :HD], (((1,), (1,)), ((), ())),
                                 preferred_element_type=F32)
        visible = lax.broadcasted_iota(jnp.int32, (1, ROWS), 1) < length
        e = jnp.where(visible, jnp.exp(scores * scale), 0.0)
        total = jnp.sum(e, axis=1, keepdims=True)
        o = jnp.dot(e.astype(BF16), kv[:, HD:], preferred_element_type=F32) / total
        cost[pl.ds(vv * gr, gr)] = o.astype(BF16).reshape(gr, R, HD)

    def co_copy(t):
        return rc(cost.at[t], cob.at[:, cols(s, HD)], co_send.at[t], co_recv.at[s], (p, t, c))

    def cross_step(i, carry):
        vv = mod(v + 1 + i, V)
        attend_cross(vv)
        for x in range(gr):
            co_copy(vv * gr + x).start()
        return carry
    lax.fori_loop(0, V - 1, cross_step, 0)
    attend_cross(v)
    for d in range(1, gr):
        co_copy(v * gr + mod(r + d, gr)).start()
    cob[:, cols(s, HD)] = cost[s]

    for d in range(1, G):
        gg = mod(g + d, G)
        wait_in(sob.at[:, cols(gg, HC)], so_recv.at[gg])
    self_ref[...] = sob[...]
    for d in range(1, n):
        t = mod(s + d, n)
        wait_in(cob.at[:, cols(t, HD)], co_recv.at[t])
    cross_ref[...] = cob[...]

    for copy, when in pending:
        if when is None:
            copy.wait_send()
        else:
            pl.when(when)(copy.wait_send)
    for d in range(1, G):
        gg = mod(g + d, G)
        rc(sost.at[gg], sob.at[:, cols(g, HC)], so_send.at[gg], so_recv.at[g],
           (p, v * gr + lax.div(gg, T), mod(gg, T))).wait_send()
    for d in range(1, n):
        co_copy(mod(s + d, n)).wait_send()


def per_device(
    video_q, video_k, video_v, cross_q, qk_gains, captions, text_gain, cross_kv_weight,
    lengths, video_prompt,
):
    parts, n, T = (lax.axis_size(a) for a in ("parts", "seq", "tp"))
    V = lengths.shape[0]
    gr = n // V
    G = gr * T
    R, DM = video_q.shape
    CR, FH = captions.shape
    HD = DM // n
    HC = DM // G
    ROWS = gr * CR
    HR = ROWS // T
    weight = cross_kv_weight.reshape(FH, 2 * HD)
    vm = pl.BlockSpec(memory_space=pltpu.VMEM)
    sm = pl.BlockSpec(memory_space=pltpu.SMEM)
    sem = pltpu.SemaphoreType.DMA
    VM = pltpu.VMEM
    return pl.pallas_call(
        functools.partial(kernel, (parts, n, T, V)),
        out_shape=(
            jax.ShapeDtypeStruct((R, DM), BF16),
            jax.ShapeDtypeStruct((R, DM), BF16),
        ),
        in_specs=[vm] * 8 + [sm] * 2,
        out_specs=(vm, vm),
        scratch_shapes=[
            VM((V, FH, 2 * HD), BF16),
            VM((gr, CR, FH), BF16),
            VM((T, ROWS, 128), F32),
            VM((ROWS, FH), BF16),
            VM((V, T, HR, 2 * HD), F32),
            VM((V, T, HR, 2 * HD), F32),
            VM((V, HR, 2 * HD), BF16),
            VM((V, T, HR, 2 * HD), BF16),
            VM((3, G, R, HC), BF16),
            VM((G, R, HC), BF16),
            VM((G, R, HC), BF16),
            VM((R, DM), BF16),
            VM((n, R, HD), BF16),
            VM((n, R, HD), BF16),
            VM((n, R, HD), BF16),
            VM((R, DM), BF16),
            sem((V, Q)), sem((V, Q)), sem((V, parts, Q)), sem((V, parts, Q)),
            sem((gr,)), sem((gr,)),
            sem((T,)), sem((T,)),
            sem((V, T)), sem((V, T)),
            sem((V,)), sem((V, T)), sem((V, T)),
            sem((3, G)), sem((3, G)),
            sem((n,)), sem((n,)),
            sem((G,)), sem((G,)),
            sem((n,)), sem((n,)),
            sem((5,)),
        ],
        compiler_params=pltpu.CompilerParams(
            collective_id=0, has_side_effects=True, vmem_limit_bytes=56 * 1024 * 1024
        ),
    )(
        video_q, video_k, video_v, cross_q, qk_gains, captions, text_gain.reshape(1, FH), weight,
        lengths, video_prompt,
    )


def solution(mesh):
    rows = P(("parts", "seq", "tp"), None)
    return jax.shard_map(
        per_device,
        mesh=mesh,
        in_specs=(
            rows, rows, rows, rows, P(), P(("parts", "seq"), "tp"), P("tp"),
            P("tp", None, "seq"), P("parts"), P("parts"),
        ),
        out_specs=(rows, rows),
        check_vma=False,
    )
```

```python
import functools
import math

import jax
import jax.numpy as jnp
from jax import lax
from jax.experimental import pallas as pl
from jax.experimental.pallas import tpu as pltpu
from jax.sharding import PartitionSpec as P

EPS = 1e-06
MESH = pl.DeviceIdType.MESH
F32, BF16 = jnp.float32, jnp.bfloat16
Q = 2


def head_norm(rows, gain):
    values = rows.astype(F32)
    inverse = lax.rsqrt(jnp.mean(values * values, axis=-1, keepdims=True) + EPS)
    return (values * inverse * gain).astype(BF16)


def kernel(
    dims, q_ref, k_ref, v_ref, cq_ref, gains_ref, cap_ref, tg_ref, w_ref, len_ref, vp_ref,
    self_ref, cross_ref,
    wbuf, capbuf, ssbuf, tn, pb, prb, kvs, kvbuf, sbuf, kn, sost, sob, cqbuf, qn, cost, cob,
    wr_send, wl_send, w_recv, f_send, cap_send, cap_recv, ss_send, ss_recv, p_send, p_recv,
    kv_send, kv_recv, kf_send, self_send, self_recv, cq_send, cq_recv,
    so_send, so_recv, co_send, co_recv, loc_sem,
):
    parts, n, T, V = dims
    gr = n // V
    G = gr * T
    p, s, c = lax.axis_index("parts"), lax.axis_index("seq"), lax.axis_index("tp")
    v, r = lax.div(s, gr), lax.rem(s, gr)
    g = r * T + c
    R, DM = q_ref.shape
    CR, FH = cap_ref.shape
    HD = DM // n
    HC = DM // G
    HL = HC // HD
    PR = FH // (parts * Q)
    ROWS = gr * CR
    HR = ROWS // T
    scale = 1.0 / math.sqrt(HD)

    def mod(a, m):
        return lax.rem(a, m)

    def rc(src, dst, ss, rs, dev):
        return pltpu.make_async_remote_copy(
            src_ref=src, dst_ref=dst, send_sem=ss, recv_sem=rs, device_id=dev, device_id_type=MESH
        )

    def cols(i, width):
        return pl.ds(pl.multiple_of(i * width, width), width)

    def prow(i, q):
        return pl.ds(pl.multiple_of((i * Q + q) * PR, PR), PR)

    left_of, right_of = v, V - 1 - v
    both = jnp.minimum(left_of, right_of)

    def nearest(k):
        near = k // 2 + 1
        far = k - both + 1
        return jnp.where(
            k < 2 * both,
            v - near if k % 2 == 0 else v + near,
            jnp.where(left_of > right_of, v - far, v + far),
        )

    barrier = pltpu.get_barrier_semaphore()
    greeted = [(p, mod(s + d, n), c) for d in range(1, n)]
    greeted += [(p, v * gr + x, mod(c + d, T)) for x in range(gr) for d in range(1, T)]
    greeted += [(mod(p + d, parts), s, c) for d in range(1, parts)]
    for dev in greeted:
        pl.semaphore_signal(barrier, inc=1, device_id=dev, device_id_type=MESH)
    own_weight = pltpu.make_async_copy(w_ref, wbuf.at[v], loc_sem.at[5])
    own_caption = pltpu.make_async_copy(cap_ref, capbuf.at[r], loc_sem.at[6])
    own_caption.start()
    own_weight.start()
    pl.semaphore_wait(barrier, len(greeted))

    pending = []

    def go(copy, when=None):
        pending.append((copy, when))
        if when is None:
            copy.start()
        else:
            pl.when(when)(copy.start)

    def wait_in(dst, sem):
        rc(dst, dst, loc_sem.at[4], sem, (p, mod(s + 1, n), c)).wait_recv()

    def pass_on(src, u, q, step, when):
        row = prow(p, q)
        target = jnp.clip(v + step, 0, V - 1) * gr + r
        sems = wr_send if step > 0 else wl_send
        go(rc(src, wbuf.at[u, row], sems.at[u, q], w_recv.at[u, p, q], (p, target, c)), when)

    for q in range(Q):
        pass_on(w_ref.at[prow(p, q)], v, q, 1, v + 1 < V)
        pass_on(w_ref.at[prow(p, q)], v, q, -1, v > 0)

    def weight_step(d, pieces=range(Q)):
        for q in pieces:
            row = prow(p, q)
            for step in (1, -1):
                there = v - step * d
                here = (there >= 0) & (there < V)
                u = jnp.clip(there, 0, V - 1)

                @pl.when(here)
                def _():
                    wait_in(wbuf.at[u, row], w_recv.at[u, p, q])
                onward = here & ((v + step >= 0) & (v + step < V))
                pass_on(wbuf.at[u, row], u, q, step, onward)
                for e in range(1, parts):
                    go(rc(wbuf.at[u, row], wbuf.at[u, row], f_send.at[u, e, q],
                          w_recv.at[u, p, q], (mod(p + e, parts), s, c)), here)

    for d in range(1, gr):
        go(rc(cap_ref, capbuf.at[r], cap_send.at[d], cap_recv.at[r],
              (p, v * gr + mod(r + d, gr), c)))
    CH = 16

    def squares(src, row0):
        def step(i, carry):
            x = src[pl.ds(pl.multiple_of(i * CH, CH), CH), :].astype(F32)
            total = jnp.sum(x * x, axis=1, keepdims=True)
            ssbuf[c, pl.ds(pl.multiple_of(row0 + i * CH, CH), CH), :] = jnp.broadcast_to(total, (CH, 128))
            return carry
        lax.fori_loop(0, CR // CH, step, 0, unroll=4)

    def normalize(src, row0):
        def step(i, carry):
            x = src[pl.ds(pl.multiple_of(i * CH, CH), CH), :].astype(F32)
            rows = pl.ds(pl.multiple_of(row0 + i * CH, CH), CH)
            total = ssbuf[0, rows, :]
            for t in range(1, T):
                total = total + ssbuf[t, rows, :]
            inverse = lax.rsqrt(total[:, :1] / (FH * T) + EPS)
            tn[rows, :] = (x * inverse * tg_ref[...]).astype(BF16)
            return carry
        lax.fori_loop(0, CR // CH, step, 0, unroll=4)

    own_caption.wait()
    squares(capbuf.at[r], r * CR)
    weight_step(1)
    for d in range(1, n):
        t = mod(s + d, n)
        go(rc(cq_ref.at[:, cols(t, HD)], cqbuf.at[s], cq_send.at[d], cq_recv.at[s], (p, t, c)))
    for d in range(2, V - 1):
        weight_step(d)
    for d in range(1, gr):
        rr = mod(r + d, gr)
        wait_in(capbuf.at[rr], cap_recv.at[rr])
        squares(capbuf.at[rr], rr * CR)
    for d in range(1, T):
        go(rc(ssbuf.at[c], ssbuf.at[c], ss_send.at[d], ss_recv.at[c], (p, s, mod(c + d, T))))
    own = []
    for a, ref in enumerate((q_ref, k_ref, v_ref)):
        for d in range(1, G):
            gg = mod(g + d, G)
            go(rc(ref.at[:, cols(gg, HC)], sbuf.at[a, g], self_send.at[a, d], self_recv.at[a, g],
                  (p, v * gr + lax.div(gg, T), mod(gg, T))))
        own.append(pltpu.make_async_copy(ref.at[:, cols(g, HC)], sbuf.at[a, g], loc_sem.at[a]))
    own.append(pltpu.make_async_copy(cq_ref.at[:, cols(s, HD)], cqbuf.at[s], loc_sem.at[3]))
    for copy in own:
        copy.start()
    for d in range(1, T):
        cc = mod(c + d, T)
        wait_in(ssbuf.at[cc], ss_recv.at[cc])
    weight_step(V - 1, range(Q // 2))
    normalize(capbuf.at[r], r * CR)
    weight_step(V - 1, range(Q // 2, Q))
    for d in range(1, gr):
        rr = mod(r + d, gr)
        normalize(capbuf.at[rr], rr * CR)

    def key_value_block(d):
        vv = v if d == 0 else nearest(d - 1)
        if d == 0:
            own_weight.wait()
        else:
            for e in range(1, parts):
                pp = mod(p + e, parts)
                for q in range(Q):
                    wait_in(wbuf.at[vv, prow(pp, q)], w_recv.at[vv, pp, q])
        weight = wbuf[vv]
        for e in range(1, T + 1):
            cc = mod(c + e, T)
            rows = pl.ds(pl.multiple_of(cc * HR, HR), HR)
            pb[d, cc] = jnp.dot(tn[rows, :], weight, preferred_element_type=F32)
            if e < T:
                go(rc(pb.at[d, cc], prb.at[d, c], p_send.at[d, e], p_recv.at[d, c], (p, s, cc)))
        total = pb[d, c]
        for e in range(1, T):
            cc = mod(c + e, T)
            wait_in(prb.at[d, cc], p_recv.at[d, cc])
            total = total + prb[d, cc]
        gain = gains_ref[3:4, cols(vv * gr + r, HD)]
        keys = head_norm(total[:, :HD], gain)
        values = total[:, HD:].astype(BF16)
        if d == 0:
            kvbuf[v, c, :, :HD] = keys
            kvbuf[v, c, :, HD:] = values
            for e in range(1, T):
                go(rc(kvbuf.at[v, c], kvbuf.at[v, c], kf_send.at[d, e], kv_recv.at[v, c],
                      (p, s, mod(c + e, T))))
        else:
            kvs[d, :, :HD] = keys
            kvs[d, :, HD:] = values
            go(rc(kvs.at[d], kvbuf.at[v, c], kv_send.at[d], kv_recv.at[v, c],
                  (p, vv * gr + r, c)))
    key_value_block(0)

    for copy in own:
        copy.wait()
    for a in (1, 0, 2):
        for d in range(1, G):
            gg = mod(g + d, G)
            wait_in(sbuf.at[a, gg], self_recv.at[a, gg])
    for j in range(HL):
        js = slice(j * HD, (j + 1) * HD)
        gain = gains_ref[1:2, cols(g * HL + j, HD)]

        def knorm(i, carry):
            kn[i, :, js] = head_norm(sbuf[1, i, :, js], gain)
            return carry
        lax.fori_loop(0, G, knorm, 0)

    def attend_self(gg):
        for j in range(HL):
            js = slice(j * HD, (j + 1) * HD)
            gain = gains_ref[0:1, cols(g * HL + j, HD)]
            queries = head_norm(sbuf[0, gg, :, js], gain)
            keys = kn[:, :, js].reshape(G * R, HD)
            scores = lax.dot_general(queries, keys, (((1,), (1,)), ((), ())),
                                     preferred_element_type=F32)
            e = jnp.exp(scores * scale)
            total = jnp.sum(e, axis=1, keepdims=True)
            values = sbuf[2, :, :, js].reshape(G * R, HD)
            o = jnp.dot(e.astype(BF16), values, preferred_element_type=F32) / total
            sost[gg, :, js] = o.astype(BF16)

    def self_step(i, carry):
        gg = mod(g + 1 + i, G)
        attend_self(gg)
        rc(sost.at[gg], sob.at[:, cols(g, HC)], so_send.at[gg], so_recv.at[g],
           (p, v * gr + lax.div(gg, T), mod(gg, T))).start()
        return carry
    lax.fori_loop(0, G - 1, self_step, 0)
    attend_self(g)
    sob[:, cols(g, HC)] = sost[g]

    for d in range(1, n):
        t = mod(s + d, n)
        wait_in(cqbuf.at[t], cq_recv.at[t])
    cross_gain = gains_ref[2:3, cols(s, HD)]

    def qnorm(i, carry):
        qn[i] = head_norm(cqbuf[i], cross_gain)
        return carry
    lax.fori_loop(0, n, qnorm, 0)

    for d in range(1, V):
        key_value_block(d)
    for d in range(1, V):
        vv = nearest(d - 1)
        wait_in(kvbuf.at[vv, c], kv_recv.at[vv, c])
        for e in range(1, T):
            go(rc(kvbuf.at[vv, c], kvbuf.at[vv, c], kf_send.at[d, e], kv_recv.at[vv, c],
                  (p, s, mod(c + e, T))))
    for d in range(V):
        vv = mod(v + V - d, V)
        for e in range(1, T):
            cc = mod(c + e, T)
            wait_in(kvbuf.at[vv, cc], kv_recv.at[vv, cc])

    def attend_cross(vv):
        prompt = vp_ref[vv]
        length = len_ref[prompt]
        kv = kvbuf[prompt].reshape(ROWS, 2 * HD)
        queries = qn[pl.ds(vv * gr, gr)].reshape(gr * R, HD)
        scores = lax.dot_general(queries, kv[:, :HD], (((1,), (1,)), ((), ())),
                                 preferred_element_type=F32)
        visible = lax.broadcasted_iota(jnp.int32, (1, ROWS), 1) < length
        e = jnp.where(visible, jnp.exp(scores * scale), 0.0)
        total = jnp.sum(e, axis=1, keepdims=True)
        o = jnp.dot(e.astype(BF16), kv[:, HD:], preferred_element_type=F32) / total
        cost[pl.ds(vv * gr, gr)] = o.astype(BF16).reshape(gr, R, HD)

    def co_copy(t):
        return rc(cost.at[t], cob.at[:, cols(s, HD)], co_send.at[t], co_recv.at[s], (p, t, c))

    def cross_step(i, carry):
        vv = mod(v + 1 + i, V)
        attend_cross(vv)
        for x in range(gr):
            co_copy(vv * gr + x).start()
        return carry
    lax.fori_loop(0, V - 1, cross_step, 0)
    attend_cross(v)
    for d in range(1, gr):
        co_copy(v * gr + mod(r + d, gr)).start()
    cob[:, cols(s, HD)] = cost[s]

    for d in range(1, G):
        gg = mod(g + d, G)
        wait_in(sob.at[:, cols(gg, HC)], so_recv.at[gg])
    self_copy = pltpu.make_async_copy(sob, self_ref, loc_sem.at[5])
    self_copy.start()
    for d in range(1, n):
        t = mod(s + d, n)
        wait_in(cob.at[:, cols(t, HD)], co_recv.at[t])
    cross_copy = pltpu.make_async_copy(cob, cross_ref, loc_sem.at[6])
    cross_copy.start()
    self_copy.wait()
    cross_copy.wait()

    for copy, when in pending:
        if when is None:
            copy.wait_send()
        else:
            pl.when(when)(copy.wait_send)
    for d in range(1, G):
        gg = mod(g + d, G)
        rc(sost.at[gg], sob.at[:, cols(g, HC)], so_send.at[gg], so_recv.at[g],
           (p, v * gr + lax.div(gg, T), mod(gg, T))).wait_send()
    for d in range(1, n):
        co_copy(mod(s + d, n)).wait_send()


def per_device(
    video_q, video_k, video_v, cross_q, qk_gains, captions, text_gain, cross_kv_weight,
    lengths, video_prompt,
):
    parts, n, T = (lax.axis_size(a) for a in ("parts", "seq", "tp"))
    V = lengths.shape[0]
    gr = n // V
    G = gr * T
    R, DM = video_q.shape
    CR, FH = captions.shape
    HD = DM // n
    HC = DM // G
    ROWS = gr * CR
    HR = ROWS // T
    weight = cross_kv_weight.reshape(FH, 2 * HD)
    vm = pl.BlockSpec(memory_space=pltpu.VMEM)
    hbm = pl.BlockSpec(memory_space=pl.ANY)
    sm = pl.BlockSpec(memory_space=pltpu.SMEM)
    sem = pltpu.SemaphoreType.DMA
    VM = pltpu.VMEM
    return pl.pallas_call(
        functools.partial(kernel, (parts, n, T, V)),
        out_shape=(
            jax.ShapeDtypeStruct((R, DM), BF16),
            jax.ShapeDtypeStruct((R, DM), BF16),
        ),
        in_specs=[hbm] * 4 + [vm, hbm, vm, hbm] + [sm] * 2,
        out_specs=(hbm, hbm),
        scratch_shapes=[
            VM((V, FH, 2 * HD), BF16),
            VM((gr, CR, FH), BF16),
            VM((T, ROWS, 128), F32),
            VM((ROWS, FH), BF16),
            VM((V, T, HR, 2 * HD), F32),
            VM((V, T, HR, 2 * HD), F32),
            VM((V, HR, 2 * HD), BF16),
            VM((V, T, HR, 2 * HD), BF16),
            VM((3, G, R, HC), BF16),
            VM((G, R, HC), BF16),
            VM((G, R, HC), BF16),
            VM((R, DM), BF16),
            VM((n, R, HD), BF16),
            VM((n, R, HD), BF16),
            VM((n, R, HD), BF16),
            VM((R, DM), BF16),
            sem((V, Q)), sem((V, Q)), sem((V, parts, Q)), sem((V, parts, Q)),
            sem((gr,)), sem((gr,)),
            sem((T,)), sem((T,)),
            sem((V, T)), sem((V, T)),
            sem((V,)), sem((V, T)), sem((V, T)),
            sem((3, G)), sem((3, G)),
            sem((n,)), sem((n,)),
            sem((G,)), sem((G,)),
            sem((n,)), sem((n,)),
            sem((7,)),
        ],
        compiler_params=pltpu.CompilerParams(
            collective_id=0, has_side_effects=True, vmem_limit_bytes=56 * 1024 * 1024
        ),
    )(
        video_q, video_k, video_v, cross_q, qk_gains, captions, text_gain.reshape(1, FH), weight,
        lengths, video_prompt,
    )


def solution(mesh):
    rows = P(("parts", "seq", "tp"), None)
    return jax.shard_map(
        per_device,
        mesh=mesh,
        in_specs=(
            rows, rows, rows, rows, P(), P(("parts", "seq"), "tp"), P("tp"),
            P("tp", None, "seq"), P("parts"), P("parts"),
        ),
        out_specs=(rows, rows),
        check_vma=False,
    )
```
